32 devices in a mesh: dp: 8 (over y, x, core), tensor: 4 (over z).
Axes of the slice: x: 2, y: 2, z: 4, core: 2. Of those that a mesh axis runs over, the one named last changes fastest.
Arguments:
- activations: bfloat16 [8192, 2560], P('dp'), may hold values from -16 to 16
- weight: bfloat16 [2560, 5120], P('dp', 'tensor'), may hold values from -0.125 to 0.125
- target: bfloat16 [8192, 5120], P('dp', 'tensor'), may hold values from -6 to 6
- start_vector: float32 [2560, 5120], P('dp', 'tensor'), may hold values from -22.9 to 22.9
- stored: float32 [4, 2560, 5120], P(None, 'dp', 'tensor'), may hold values from -6.8 to 6.8
Outputs:
- krylov: float32 [2, 2560, 5120], P(None, 'dp', 'tensor')
- coef_first: float32 [6], replicated
- coef_second: float32 [7], replicated
- projections: float32 [16, 7], P('dp')
The draws below stay inside these ranges and needn't reach their ends.
All inputs are finite; a program needn't handle non-finite values.
Results may differ from the reference program's by a relative error of at most 0.0052.
Values may be sent and summed in bfloat16 or wider, within the bound.
A program may use at most 320 MiB of HBM per device.

```python
import math
import jax
import jax.numpy as jnp
from jax import lax

A = 2560
D = 5120
KS = 4
ITERS = 2
TOKENS = 8192
EXAMPLES = 16
TOK_EX = 512


def draw_activations(key, part):
    key_values, key_scales = jax.random.split(key)
    columns_pos = jnp.arange(A, dtype=jnp.float32) / A
    rows_pos = jnp.arange(TOKENS, dtype=jnp.float32) / TOKENS
    values = jnp.clip(jax.random.normal(key_values, (TOKENS, A), jnp.float32), -4.0, 4.0)
    column_rand = jnp.exp(jax.random.uniform(key_scales, (A,), jnp.float32, math.log(0.5), math.log(2.0)))
    column_trend = jnp.exp(math.log(3.0) * columns_pos)
    row_trend = jnp.exp(math.log(2.0) * rows_pos)
    scaled = values * (column_trend * column_rand)[None, :] * row_trend[:, None] / 3.0
    return scaled.astype(jnp.bfloat16)


def basis_arrays(key):
    base_key = jax.random.fold_in(key, 41)

    def one_array(number):
        array_key = jax.random.fold_in(base_key, number)
        return jnp.clip(jax.random.normal(array_key, (A, D), jnp.float32), -4.0, 4.0)
    common = one_array(0)
    members = [one_array(number + 1) for number in range(KS)]
    own_part = one_array(KS + 1)
    return (common, members, own_part)


def draw_stored(key, part):
    common, members, own_part = basis_arrays(key)
    return jnp.stack([member + 0.7 * common for member in members])


def draw_start_vector(key, part):
    common, members, own_part = basis_arrays(key)
    mixture = own_part + 0.7 * common
    for member in members:
        mixture = mixture + 0.4 * member
    position = jnp.arange(A, dtype=jnp.float32) / A
    trend = jnp.exp(math.log(3.0) * (position - 0.5))[:, None]
    return mixture * trend


def block_scale(rng, extent, cuts, smallest, top_value):
    def one(dim, shards_of):
        steps = jax.random.uniform(jax.random.fold_in(jax.random.fold_in(rng, 6), dim), (shards_of,), jnp.float32, smallest / len(cuts), top_value / len(cuts))
        return jnp.repeat(jnp.exp(steps), extent[dim] // shards_of).reshape((-1,) + (1,) * (len(extent) - dim - 1))

    level = one(*cuts[0])
    for cut in cuts[1:]:
        level = level * one(*cut)
    return level


def gaussian(stream_key, dims, width, bound, pieces=(), held_as=jnp.bfloat16):
    array = jax.random.normal(stream_key, dims, jnp.float32) * width
    if len(pieces) > 0:
        array = block_scale(stream_key, dims, pieces, -0.22, 0.18) * array
    return jnp.clip(array, min=-bound, max=bound).astype(held_as)


def setup_inputs(seed: int = 0) -> dict:
    key_of = jax.random.split(jax.random.key(seed), 6)
    return {
        "activations": draw_activations(jax.random.fold_in(key_of[5], 71), 0),
        "weight": gaussian(key_of[1], (A, D), A ** -0.5, 0.125, ((0, 8), (1, 4))),
        "target": gaussian(key_of[2], (TOKENS, D), 1.0, 6.0, ((0, 8), (1, 4))),
        "start_vector": draw_start_vector(jax.random.fold_in(key_of[5], 71), 0),
        "stored": draw_stored(jax.random.fold_in(key_of[5], 71), 0),
    }


def reference(activations, weight, target, start_vector, stored):
    nparam = float(A * D)
    hidden = jnp.dot(activations, weight, preferred_element_type=jnp.float32)
    slope = jnp.tanh(hidden - target.astype(jnp.float32))
    curvature = (1.0 - slope * slope) / TOKENS

    def inner_product(left, right):
        return jnp.sum(left * right) / nparam

    def hessian_product(vector):
        direction = vector.astype(jnp.bfloat16)
        mapped = jnp.dot(activations, direction, preferred_element_type=jnp.float32)
        scaled = (curvature * mapped).astype(jnp.bfloat16)
        return jnp.dot(activations.T, scaled, preferred_element_type=jnp.float32)
    basis = [stored[position] for position in range(KS)]
    basis.append(start_vector / jnp.sqrt(inner_product(start_vector, start_vector)))
    columns = []
    for iteration in range(ITERS):
        imaged = hessian_product(basis[-1])
        first_coef = jnp.stack([inner_product(vector, imaged) for vector in basis])
        remainder = imaged
        for position in range(len(basis)):
            remainder = remainder - first_coef[position] * basis[position]
        second = jnp.stack([inner_product(vector, remainder) for vector in basis])
        for position in range(len(basis)):
            remainder = remainder - second[position] * basis[position]
        length_norm = jnp.sqrt(inner_product(remainder, remainder))
        columns.append(jnp.concatenate([first_coef + second, length_norm[None]]))
        basis.append(remainder / length_norm)
    krylov = jnp.stack(basis[KS + 1:])
    signs = slope.astype(jnp.bfloat16)
    basis_table = jnp.stack([vector.astype(jnp.bfloat16) for vector in basis]).reshape(len(basis), A * D)

    def one_example(example):
        rows = lax.dynamic_slice_in_dim(activations, example * TOK_EX, TOK_EX, 0)
        errors = lax.dynamic_slice_in_dim(signs, example * TOK_EX, TOK_EX, 0)
        grad = jnp.dot(rows.T, errors, preferred_element_type=jnp.float32).astype(jnp.bfloat16)
        return jnp.dot(basis_table, grad.reshape(A * D), preferred_element_type=jnp.float32)
    projections = lax.map(one_example, jnp.arange(EXAMPLES, dtype=jnp.int32))
    projections = projections / math.sqrt(float(TOK_EX) * nparam)
    return (krylov, columns[0], columns[1], projections)
```

```python
import math

import jax
import jax.numpy as jnp
from jax import lax
from jax.sharding import PartitionSpec as P

ITERS = 2
BOTH = ("dp", "tensor")


def dots(vectors, one):
    return [jnp.sum(v * one) for v in vectors]


def orthogonalize(vectors, imaged, firsts, square, gram):
    second = firsts - jnp.sum(gram * firsts[None, :], axis=1)
    total = firsts + second
    rest = square - 2.0 * jnp.sum(total * firsts) + jnp.sum(
        total[:, None] * gram * total[None, :]
    )
    norm = jnp.sqrt(rest)
    remainder = imaged
    for k, v in enumerate(vectors):
        remainder = remainder - total[k] * v
    return remainder / norm, jnp.concatenate([total, norm[None]])


def shards(activations, weight, target, start_vector, stored):
    rows = activations.shape[0]
    ndp = lax.axis_size("dp")
    total_rows = rows * ndp
    nparam = float(weight.shape[0] * ndp * weight.shape[1] * lax.axis_size("tensor"))
    tok_ex = 512
    examples = rows // tok_ex
    ks = stored.shape[0]

    square_sum = lax.psum(jnp.sum(start_vector * start_vector), BOTH) / nparam
    q0 = start_vector / jnp.sqrt(square_sum)
    full_weight, q0 = lax.optimization_barrier(
        (lax.all_gather(weight, "dp", axis=0, tiled=True), q0)
    )
    hidden = jnp.dot(activations, full_weight, preferred_element_type=jnp.float32)
    slope = jnp.tanh(hidden - target.astype(jnp.float32))
    curvature = (1.0 - slope * slope) / total_rows
    signs = slope.astype(jnp.bfloat16)

    def project(mapped):
        part = signs.astype(jnp.float32) * mapped
        return jnp.sum(part.reshape(examples, -1), axis=1)

    def gather(v):
        return lax.all_gather(v, "dp", axis=v.ndim - 2, tiled=True)

    def image(v):
        return jnp.dot(activations, v, preferred_element_type=jnp.float32)

    def hessian(v):
        mapped = image(gather(v.astype(jnp.bfloat16)))
        scaled = (curvature * mapped).astype(jnp.bfloat16)
        part = jnp.dot(activations.T, scaled, preferred_element_type=jnp.float32)
        imaged = lax.psum_scatter(part, "dp", scatter_dimension=0, tiled=True)
        return imaged, project(mapped)

    vectors = [stored[k] for k in range(ks)] + [q0]
    table = stored.astype(jnp.bfloat16)
    half = ks // 2

    w, proj_q0 = hessian(q0)
    gram_local = []
    for i in range(ks + 1):
        for j in range(i + 1):
            gram_local.append(jnp.sum(vectors[i] * vectors[j]))
    table_a, _ = lax.optimization_barrier((table[:half], w[0, 0]))
    full_a = gather(table_a)
    sums = lax.psum(
        jnp.stack(dots(vectors, w) + [jnp.sum(w * w)] + gram_local), BOTH
    ) / nparam
    n = ks + 1
    index = [[0] * n for _ in range(n)]
    count = 0
    for i in range(n):
        for j in range(i + 1):
            index[i][j] = index[j][i] = n + 1 + count
            count += 1
    gram = jnp.stack([jnp.stack([sums[index[i][j]] for j in range(n)]) for i in range(n)])
    q1, coef_first = orthogonalize(vectors, w, sums[:n], sums[n], gram)

    w, proj_q1 = hessian(q1)
    cross_local = dots(vectors, q1) + [jnp.sum(q1 * q1)]
    vectors = vectors + [q1]
    table_b, _ = lax.optimization_barrier((table[half:], w[0, 0]))
    full_b = gather(table_b)
    m = n + 1
    sums = lax.psum(
        jnp.stack(dots(vectors, w) + [jnp.sum(w * w)] + cross_local), BOTH
    ) / nparam
    cross = sums[m + 1 :]
    gram = jnp.concatenate(
        [jnp.concatenate([gram, cross[:n, None]], axis=1), cross[None, :]], axis=0
    )
    q2, coef_second = orthogonalize(vectors, w, sums[:m], sums[m], gram)

    parts = [project(image(full_a[k])) for k in range(half)]
    parts += [project(image(full_b[k])) for k in range(ks - half)]
    parts += [proj_q0, proj_q1, project(image(gather(q2.astype(jnp.bfloat16))))]
    projections = lax.psum(jnp.stack(parts, axis=1), "tensor")
    projections = projections / math.sqrt(float(tok_ex) * nparam)
    return (jnp.stack([q1, q2]), coef_first, coef_second, projections)


def solution(mesh):
    in_specs = (
        P("dp", None),
        P("dp", "tensor"),
        P("dp", "tensor"),
        P("dp", "tensor"),
        P(None, "dp", "tensor"),
    )
    out_specs = (P(None, "dp", "tensor"), P(), P(), P("dp", None))
    return jax.shard_map(shards, mesh=mesh, in_specs=in_specs, out_specs=out_specs, check_vma=False)
```

```python
import math

import jax
import jax.numpy as jnp
from jax import lax
from jax.sharding import PartitionSpec as P

ITERS = 2
BOTH = ("dp", "tensor")


def dots(vectors, one):
    return jnp.sum(jnp.stack(vectors) * one[None], axis=(1, 2))


def orthogonalize(vectors, imaged, firsts, square, gram):
    second = firsts - jnp.sum(gram * firsts[None, :], axis=1)
    total = firsts + second
    rest = square - 2.0 * jnp.sum(total * firsts) + jnp.sum(
        total[:, None] * gram * total[None, :]
    )
    norm = jnp.sqrt(rest)
    remainder = imaged
    for k, v in enumerate(vectors):
        remainder = remainder - total[k] * v
    return remainder / norm, jnp.concatenate([total, norm[None]])


def shards(activations, weight, target, start_vector, stored):
    rows = activations.shape[0]
    ndp = lax.axis_size("dp")
    total_rows = rows * ndp
    nparam = float(weight.shape[0] * ndp * weight.shape[1] * lax.axis_size("tensor"))
    tok_ex = 512
    examples = rows // tok_ex
    ks = stored.shape[0]

    square_sum = lax.psum(jnp.sum(start_vector * start_vector), BOTH) / nparam
    q0 = start_vector / jnp.sqrt(square_sum)
    full_weight, q0 = lax.optimization_barrier(
        (lax.all_gather(weight, "dp", axis=0, tiled=True), q0)
    )
    hidden = jnp.dot(activations, full_weight, preferred_element_type=jnp.float32)
    slope = jnp.tanh(hidden - target.astype(jnp.float32))
    curvature = (1.0 - slope * slope) / total_rows
    signs = slope.astype(jnp.bfloat16)

    def project(mapped):
        part = signs.astype(jnp.float32) * mapped
        return jnp.sum(part.reshape(examples, -1), axis=1)

    def gather(v):
        return lax.all_gather(v, "dp", axis=v.ndim - 2, tiled=True)

    def image(v):
        return jnp.dot(activations, v, preferred_element_type=jnp.float32)

    def hessian(v):
        mapped = image(gather(v.astype(jnp.bfloat16)))
        scaled = (curvature * mapped).astype(jnp.bfloat16)
        part = jnp.dot(activations.T, scaled, preferred_element_type=jnp.float32)
        imaged = lax.psum_scatter(
            part.astype(jnp.bfloat16), "dp", scatter_dimension=0, tiled=True
        )
        return imaged.astype(jnp.float32), project(mapped)

    vectors = [stored[k] for k in range(ks)] + [q0]
    table = stored.astype(jnp.bfloat16)
    half = ks // 2

    w, proj_q0 = hessian(q0)
    n = ks + 1
    table_a, _ = lax.optimization_barrier((table[:half], w[0, 0]))
    full_a = gather(table_a)
    gram_rows = [dots(vectors, v) for v in vectors]
    sums = lax.psum(jnp.concatenate([dots(vectors + [w], w)] + gram_rows), BOTH) / nparam
    gram = sums[n + 1 :].reshape(n, n)
    q1, coef_first = orthogonalize(vectors, w, sums[:n], sums[n], gram)

    full_a, q1 = lax.optimization_barrier((full_a, q1))
    vectors = vectors + [q1]
    w, proj_q1 = hessian(q1)
    cross = dots(vectors, q1)
    m = n + 1
    table_b, _ = lax.optimization_barrier((table[half:], w[0, 0]))
    full_b = gather(table_b)
    sums = lax.psum(jnp.concatenate([dots(vectors + [w], w), cross]), BOTH) / nparam
    cross = sums[m + 1 :]
    gram = jnp.concatenate(
        [jnp.concatenate([gram, cross[:n, None]], axis=1), cross[None, :]], axis=0
    )
    q2, coef_second = orthogonalize(vectors, w, sums[:m], sums[m], gram)
    full_b, q2 = lax.optimization_barrier((full_b, q2))

    parts = [project(image(full_a[k])) for k in range(half)]
    parts += [project(image(full_b[k])) for k in range(ks - half)]
    parts += [proj_q0, proj_q1, project(image(gather(q2.astype(jnp.bfloat16))))]
    projections = lax.psum(jnp.stack(parts, axis=1), "tensor")
    projections = projections / math.sqrt(float(tok_ex) * nparam)
    return (jnp.stack([q1, q2]), coef_first, coef_second, projections)


def solution(mesh):
    in_specs = (
        P("dp", None),
        P("dp", "tensor"),
        P("dp", "tensor"),
        P("dp", "tensor"),
        P(None, "dp", "tensor"),
    )
    out_specs = (P(None, "dp", "tensor"), P(), P(), P("dp", None))
    return jax.shard_map(shards, mesh=mesh, in_specs=in_specs, out_specs=out_specs, check_vma=False)
```

```python
import math

import jax
import jax.numpy as jnp
from jax import lax
from jax.sharding import PartitionSpec as P

ITERS = 2
BOTH = ("dp", "tensor")


def dots(vectors, one):
    return jnp.sum(jnp.stack(vectors) * one[None], axis=(1, 2))


def orthogonalize(vectors, imaged, firsts, square, gram):
    second = firsts - jnp.sum(gram * firsts[None, :], axis=1)
    total = firsts + second
    rest = square - 2.0 * jnp.sum(total * firsts) + jnp.sum(
        total[:, None] * gram * total[None, :]
    )
    norm = jnp.sqrt(rest)
    remainder = imaged
    for k, v in enumerate(vectors):
        remainder = remainder - total[k] * v
    return remainder / norm, jnp.concatenate([total, norm[None]])


def shards(activations, weight, target, start_vector, stored):
    rows = activations.shape[0]
    ndp = lax.axis_size("dp")
    total_rows = rows * ndp
    nparam = float(weight.shape[0] * ndp * weight.shape[1] * lax.axis_size("tensor"))
    tok_ex = 512
    examples = rows // tok_ex
    ks = stored.shape[0]

    square_sum = lax.psum(jnp.sum(start_vector * start_vector), BOTH) / nparam
    q0 = start_vector / jnp.sqrt(square_sum)
    full_weight, q0 = lax.optimization_barrier(
        (lax.all_gather(weight, "dp", axis=0, tiled=True), q0)
    )
    hidden = jnp.dot(activations, full_weight, preferred_element_type=jnp.float32)
    slope = jnp.tanh(hidden - target.astype(jnp.float32))
    curvature = (1.0 - slope * slope) / total_rows
    signs = slope.astype(jnp.bfloat16)

    def project(mapped):
        part = signs.astype(jnp.float32) * mapped
        return jnp.sum(part.reshape(examples, -1), axis=1)

    def gather(v):
        return lax.all_gather(v, "dp", axis=v.ndim - 2, tiled=True)

    def image(v):
        return jnp.dot(activations, v, preferred_element_type=jnp.float32)

    def hessian(v, piece, ready=()):
        full = gather(v.astype(jnp.bfloat16))
        ready = [project(image(u)) for u in ready]
        piece, full, ready = lax.optimization_barrier((piece, full, ready))
        full_piece = gather(piece)
        mapped = image(full)
        scaled = (curvature * mapped).astype(jnp.bfloat16)
        part = jnp.dot(activations.T, scaled, preferred_element_type=jnp.float32)
        part, full_piece = lax.optimization_barrier(
            (part.astype(jnp.bfloat16), full_piece)
        )
        imaged = lax.psum_scatter(part, "dp", scatter_dimension=0, tiled=True)
        return imaged, project(mapped), full_piece, ready

    def reduce_beside(local, done):
        local, done = lax.optimization_barrier((local, done))
        return lax.psum(local, BOTH) / nparam, done

    vectors = [stored[k] for k in range(ks)] + [q0]
    table = stored.astype(jnp.bfloat16)
    cuts = [1, ks - 1]
    n = ks + 1
    m = n + 1

    w, proj_q0, piece, _ = hessian(q0, table[: cuts[0]])
    table_a, _ = lax.optimization_barrier((table[cuts[0] : cuts[1]], w[0, 0]))
    full_a = gather(table_a)
    done = [project(image(v)) for v in piece]
    w = w.astype(jnp.float32)
    gram_rows = [dots(vectors, v) for v in vectors]
    sums, done = reduce_beside(jnp.concatenate([dots(vectors + [w], w)] + gram_rows), done)
    gram = sums[n + 1 :].reshape(n, n)
    q1, coef_first = orthogonalize(vectors, w, sums[:n], sums[n], gram)

    full_a, q1 = lax.optimization_barrier((full_a, q1))
    vectors = vectors + [q1]
    w_sent, proj_q1, piece, ready = hessian(q1, table[cuts[1] :], full_a)
    cross = dots(vectors, q1)
    done = done + list(ready) + [project(image(v)) for v in piece]
    w_sent, done, cross = lax.optimization_barrier((w_sent, done, cross))
    full_w = gather(w_sent)
    w = w_sent.astype(jnp.float32)
    sums, done = reduce_beside(jnp.concatenate([dots(vectors + [w], w), cross]), done)
    cross = sums[m + 1 :]
    gram = jnp.concatenate(
        [jnp.concatenate([gram, cross[:n, None]], axis=1), cross[None, :]], axis=0
    )
    q2, coef_second = orthogonalize(vectors, w, sums[:m], sums[m], gram)

    parts = done + [proj_q0, proj_q1]
    last = project(image(full_w))
    for k in range(m):
        last = last - coef_second[k] * parts[k]
    parts = parts + [last / coef_second[m]]
    projections = lax.psum(jnp.stack(parts, axis=1), "tensor")
    projections = projections / math.sqrt(float(tok_ex) * nparam)
    return (jnp.stack([q1, q2]), coef_first, coef_second, projections)


def solution(mesh):
    in_specs = (
        P("dp", None),
        P("dp", "tensor"),
        P("dp", "tensor"),
        P("dp", "tensor"),
        P(None, "dp", "tensor"),
    )
    out_specs = (P(None, "dp", "tensor"), P(), P(), P("dp", None))
    return jax.shard_map(shards, mesh=mesh, in_specs=in_specs, out_specs=out_specs, check_vma=False)
```
